32 devices in a mesh: groups: 2 (over y), inp: 2 (over x), outp: 4 (over z), depth: 2 (over core).
Axes of the slice: x: 2, y: 2, z: 4, core: 2. Of those that a mesh axis runs over, the one named last changes fastest.
Arguments:
- tokens: bfloat16 [1024, 5120], P(('groups', 'depth', 'outp'), 'inp'), parts along dimension 0, may hold values from -6 to 6
- gate_pre: bfloat16 [1024, 16384], P(('groups', 'depth', 'inp'), 'outp'), parts along dimension 0, may hold values from -8 to 8
- up_pre: bfloat16 [1024, 16384], P(('groups', 'depth', 'inp'), 'outp'), parts along dimension 0, may hold values from -6 to 6
- grad_hidden: bfloat16 [1024, 16384], P(('groups', 'depth', 'inp'), 'outp'), parts along dimension 0, may hold values from -2.109375 to 2.109375
- gate_weight: bfloat16 [5120, 16384], P('inp', ('outp', 'depth')), may hold values from -0.078125 to 0.078125
- up_weight: bfloat16 [5120, 16384], P('inp', ('outp', 'depth')), may hold values from -0.078125 to 0.078125
Outputs:
- grad_tokens: bfloat16 [1024, 5120], P(('groups', 'depth', 'outp'), 'inp'), parts along dimension 0
- grad_gate_weight: bfloat16 [10240, 16384], P(('groups', 'inp'), ('outp', 'depth')), parts along dimension 0
- grad_up_weight: bfloat16 [10240, 16384], P(('groups', 'inp'), ('outp', 'depth')), parts along dimension 0
The draws below stay inside these ranges and needn't reach their ends.
There are 2 independent parts, one for each index of `groups`. The reference program is written for one: setup_inputs(seed, part) draws one part's arguments, and reference() takes and returns one part's arrays. A program takes and returns all parts, laid end to end along the dimension named above; an argument that names none is the same for every part. Nothing has to cross between parts.
All inputs are finite; a program needn't handle non-finite values.
Results may differ from the reference program's by a relative error of at most 0.0059.
Values may be sent and summed in bfloat16 or wider, within the bound.
A program may use at most 256 MiB of HBM per device.

```python
import jax
import jax.numpy as jnp
from jax import lax

D = 5120
FF = 16384
TOK_DEV = 256
TOKENS = 512


def block_scale(stream_key, extent, shards, least, largest):
    gain, own = 1.0, jax.random.fold_in(stream_key, 6)
    for dim, parts in shards:
        steps = jnp.exp(jax.random.uniform(jax.random.fold_in(own, dim), (parts,), jnp.float32, least / len(shards), largest / len(shards)))
        gain = gain * jnp.repeat(steps, extent[dim] // parts).reshape([-1 if axis == dim else 1 for axis in range(len(extent))])
    return gain


def gaussian(own_key, extent, scale, reach, shards=(), held_as=jnp.bfloat16):
    entries = jax.random.normal(own_key, extent, jnp.float32) * scale
    if len(shards) > 0:
        entries = block_scale(own_key, extent, shards, -0.22, 0.18) * entries
    return jnp.clip(entries, min=-reach, max=reach).astype(held_as)


def setup_inputs(seed: int = 0, part: int = 0) -> dict:
    streams_of = jax.random.split(jax.random.key(seed), 7)
    part_keys = jax.random.split(jax.random.fold_in(streams_of[6], part), 7)
    return {
        "tokens": gaussian(part_keys[0], (TOKENS, D), 1.0, 6.0, ((0, 8), (1, 2))),
        "gate_pre": gaussian(part_keys[1], (TOKENS, FF), 1.5, 8.0, ((0, 4), (1, 4))),
        "up_pre": gaussian(part_keys[2], (TOKENS, FF), 1.0, 6.0, ((0, 4), (1, 4))),
        "grad_hidden": gaussian(part_keys[3], (TOKENS, FF), (6.0 * TOKENS ** -0.5), 2.109375, ((0, 4), (1, 4))),
        "gate_weight": gaussian(streams_of[4], (D, FF), D ** -0.5, 0.078125, ((0, 2), (1, 8))),
        "up_weight": gaussian(streams_of[5], (D, FF), D ** -0.5, 0.078125, ((0, 2), (1, 8))),
    }


def reference(tokens, gate_pre, up_pre, grad_hidden, gate_weight, up_weight):
    g = gate_pre.astype(jnp.float32)
    u = up_pre.astype(jnp.float32)
    h = grad_hidden.astype(jnp.float32)
    s = jax.nn.sigmoid(g)
    grad_up = (h * g * s).astype(jnp.bfloat16)
    grad_gate = (h * u * s * (1.0 + g * (1.0 - s))).astype(jnp.bfloat16)
    back = jnp.dot(grad_gate, gate_weight.T, preferred_element_type=jnp.float32)
    back = back + jnp.dot(grad_up, up_weight.T, preferred_element_type=jnp.float32)
    grad_tokens = back.astype(jnp.bfloat16)
    total_gate = jnp.zeros((D, FF), jnp.float32)
    total_up = jnp.zeros((D, FF), jnp.float32)
    for block in range(TOKENS // TOK_DEV):
        rows = tokens[block * TOK_DEV:(block + 1) * TOK_DEV]
        part_gate = jnp.dot(rows.T, grad_gate[block * TOK_DEV:(block + 1) * TOK_DEV], preferred_element_type=jnp.float32)
        part_up = jnp.dot(rows.T, grad_up[block * TOK_DEV:(block + 1) * TOK_DEV], preferred_element_type=jnp.float32)
        total_gate = total_gate + lax.optimization_barrier(part_gate.astype(jnp.bfloat16)).astype(jnp.float32)
        total_up = total_up + lax.optimization_barrier(part_up.astype(jnp.bfloat16)).astype(jnp.float32)
    return grad_tokens, total_gate.astype(jnp.bfloat16), total_up.astype(jnp.bfloat16)
```

```python
import functools

import jax
import jax.numpy as jnp
from jax import lax
from jax.experimental import pallas as pl
from jax.experimental.pallas import tpu as pltpu
from jax.sharding import PartitionSpec as P

MESH = pl.DeviceIdType.MESH
f32, bf16 = jnp.float32, jnp.bfloat16
VMEM_BYTES = 60 * 1024 * 1024


def width(extent):
    return 256 if extent % 256 == 0 else 128


def exchange(
    n_inp, n_outp,
    tokens, gate, up, hidden, w_gate, w_up,
    out, grads_out, turned_out,
    gv, uv, hv, wg, wu, tk, turned, gr, sb, pf, pb, xr, zs, zr, ov,
    in_sem, own_sem, w_sem, t_send, t_recv, f_send, f_recv,
    g_send, g_recv, x_send, x_recv, z_send, z_recv, o_sem, out_sem,
):
    i, o, d = lax.axis_index("inp"), lax.axis_index("outp"), lax.axis_index("depth")
    e = 1 - d
    rows, feats = tokens.shape
    per = gate.shape[0] // rows
    half = gate.shape[1] // 2
    inps = [lax.rem(i + s, n_inp) for s in range(n_inp)]
    outps = [lax.rem(o + s, n_outp) for s in range(n_outp)]

    loads = []
    for p in range(per):
        part = pl.ds(p * rows, rows)
        loads.append([
            pltpu.make_async_copy(src.at[part], dst.at[part], in_sem.at[p, k])
            for k, (src, dst) in enumerate(((gate, gv), (up, uv), (hidden, hv)))
        ])
    own = pltpu.make_async_copy(tokens, tk.at[o, d], own_sem)
    weights = [
        pltpu.make_async_copy(w_gate, wg, w_sem.at[0]),
        pltpu.make_async_copy(w_up, wu, w_sem.at[1]),
    ]
    for copy in loads[0] + [own] + sum(loads[1:], []) + weights:
        copy.start()

    barrier = pltpu.get_barrier_semaphore()
    for s in range(n_inp):
        for q in ((e,) if s == 0 else (d, e)):
            pl.semaphore_signal(barrier, inc=1, device_id={"inp": inps[s], "depth": q}, device_id_type=MESH)
    for s in range(1, n_outp):
        pl.semaphore_signal(barrier, inc=1, device_id={"outp": outps[s]}, device_id_type=MESH)
    pl.semaphore_wait(barrier, 2 * n_inp - 1 + n_outp - 1)

    cw = width(half)

    def pointwise(p, side, store):
        def step(c, carry):
            at = (pl.ds(p * rows, rows), pl.ds(pl.multiple_of(side * half + c * cw, cw), cw))
            g, u, h = gv[at].astype(f32), uv[at].astype(f32), hv[at].astype(f32)
            sig = 1.0 / (1.0 + jnp.exp(-g))
            hs = h * sig
            cols = pl.ds(pl.multiple_of(c * cw, cw), cw)
            store(cols, (hs * u * (1.0 + g * (1.0 - sig))).astype(bf16), (hs * g).astype(bf16))
            return carry
        lax.fori_loop(0, half // cw, step, 0)

    def grad_copy(p, s, q, src):
        slot = gr.at[:, i * per + p, d]
        return pltpu.make_async_remote_copy(
            src_ref=src, dst_ref=slot,
            send_sem=g_send.at[s, q, p], recv_sem=g_recv.at[i, d, p],
            device_id={"inp": inps[s], "depth": d if q == 0 else e}, device_id_type=MESH,
        )

    sends = []
    for p in range(per):
        for copy in loads[p]:
            copy.wait()
        mine = i * per + p

        def store_there(cols, a, b):
            sb[0, p, :, cols] = a
            sb[1, p, :, cols] = b

        def store_here(cols, a, b):
            gr[0, mine, d, :, cols] = a
            gr[1, mine, d, :, cols] = b

        pointwise(p, e, store_there)
        for s in list(range(1, n_inp)) + [0]:
            copy = grad_copy(p, s, 1, sb.at[:, p])
            copy.start()
            sends.append(copy)
        pointwise(p, d, store_here)
        for s in range(1, n_inp):
            copy = grad_copy(p, s, 0, gr.at[:, mine, d])
            copy.start()
            sends.append(copy)
        if p == 0:
            own.wait()
            for s in range(1, n_outp):
                copy = pltpu.make_async_remote_copy(
                    src_ref=tk.at[o, d], dst_ref=tk.at[o, d],
                    send_sem=t_send.at[s], recv_sem=t_recv.at[o],
                    device_id={"outp": outps[s]}, device_id_type=MESH,
                )
                copy.start()
                sends.append(copy)

    def await_grads(j, q, p):
        slot = gr.at[:, j * per + p, q]
        pltpu.make_async_remote_copy(
            src_ref=slot, dst_ref=slot, send_sem=g_send.at[0, 0, 0], recv_sem=g_recv.at[j, q, p],
            device_id={"depth": e}, device_id_type=MESH,
        ).wait_recv()

    fw = width(feats)

    def product(c):
        left_gate = gr[0, c].reshape(2 * rows, half)
        left_up = gr[1, c].reshape(2 * rows, half)

        def step(t, carry):
            cols = pl.ds(pl.multiple_of(t * fw, fw), fw)
            contract = (((1,), (1,)), ((), ()))
            acc = lax.dot_general(left_gate, wg[cols, :], contract, preferred_element_type=f32)
            acc = acc + lax.dot_general(left_up, wu[cols, :], contract, preferred_element_type=f32)
            acc = acc.reshape(2, rows, fw)
            pf[c, :, :, cols] = acc
            pb[c, :, :, cols] = acc.astype(bf16)
            return carry
        lax.fori_loop(0, feats // fw, step, 0)

    def pair_copy(c):
        return pltpu.make_async_remote_copy(
            src_ref=pb.at[c, e], dst_ref=xr.at[c], send_sem=x_send.at[c], recv_sem=x_recv.at[c],
            device_id={"depth": e}, device_id_type=MESH,
        )

    def store_grads(c):
        return pltpu.make_async_copy(gr.at[:, c], grads_out.at[:, c], o_sem.at[c])

    def spread_copy(c):
        return pltpu.make_async_remote_copy(
            src_ref=zs.at[c], dst_ref=zr.at[o], send_sem=z_send.at[c], recv_sem=z_recv.at[o],
            device_id={"outp": c}, device_id_type=MESH,
        )

    def begin(c):
        product(c)
        pair_copy(c).start()
        store_grads(c).start()

    def spread(c):
        pair_copy(c).wait_recv()
        summed = (pf[c, d] + xr[c].astype(f32)).astype(bf16)

        @pl.when(c != o)
        def _():
            zs[c] = summed
            spread_copy(c).start()

        @pl.when(c == o)
        def _():
            zr[o] = summed

    for p in range(per):
        await_grads(i, e, p)
    for copy in weights:
        copy.wait()
    for p in range(per):
        begin(i * per + p)
    for p in range(per):
        spread(i * per + p)

    def take_tokens():
        for s in range(1, n_outp):
            pltpu.make_async_remote_copy(
                src_ref=tk.at[outps[s], d], dst_ref=tk.at[outps[s], d],
                send_sem=t_send.at[0], recv_sem=t_recv.at[outps[s]],
                device_id={"depth": e}, device_id_type=MESH,
            ).wait_recv()
        onward = pltpu.make_async_remote_copy(
            src_ref=tk.at[:, d], dst_ref=tk.at[:, d], send_sem=f_send, recv_sem=f_recv,
            device_id={"depth": e}, device_id_type=MESH,
        )
        onward.start()
        pltpu.make_async_remote_copy(
            src_ref=tk.at[:, e], dst_ref=tk.at[:, e], send_sem=f_send, recv_sem=f_recv,
            device_id={"depth": e}, device_id_type=MESH,
        ).wait_recv()

        def step(t, carry):
            cols = pl.ds(pl.multiple_of(t * fw, fw), fw)
            turned[cols, :] = tk[:, :, :, cols].reshape(n_outp * 2 * rows, fw).T
            return carry
        lax.fori_loop(0, feats // fw, step, 0)
        result = pltpu.make_async_copy(turned, turned_out, out_sem.at[0])
        result.start()
        return onward, result

    later = [(s, p) for s in range(1, n_inp) for p in range(per)]
    onward = turned_copy = None
    for at, (s, p) in enumerate(later):
        if at == len(later) - 1:
            onward, turned_copy = take_tokens()
        for q in (d, e):
            await_grads(inps[s], q, p)
        begin(inps[s] * per + p)
        spread(inps[s] * per + p)

    for s in range(1, n_outp):
        pltpu.make_async_remote_copy(
            src_ref=zr.at[outps[s]], dst_ref=zr.at[outps[s]],
            send_sem=z_send.at[0], recv_sem=z_recv.at[outps[s]],
            device_id={"depth": e}, device_id_type=MESH,
        ).wait_recv()

    def total(t, carry):
        cols = pl.ds(pl.multiple_of(t * fw, fw), fw)
        acc = zr[0, :, cols].astype(f32)
        for c in range(1, n_outp):
            acc = acc + zr[c, :, cols].astype(f32)
        ov[:, cols] = acc.astype(bf16)
        return carry
    lax.fori_loop(0, feats // fw, total, 0)
    result = pltpu.make_async_copy(ov, out, out_sem.at[1])
    result.start()

    for copy in sends:
        copy.wait_send()
    onward.wait_send()
    for c in range(n_outp):
        pair_copy(c).wait_send()
        store_grads(c).wait()

        @pl.when(c != o)
        def _():
            spread_copy(c).wait_send()
    turned_copy.wait()
    result.wait()


def weight_grads(turned, grads, out_gate, out_up):
    left = turned[...]
    cw = width(out_gate.shape[1])
    for c in range(out_gate.shape[1] // cw):
        cols = slice(c * cw, (c + 1) * cw)
        out_gate[:, cols] = jnp.dot(left, grads[0, :, cols], preferred_element_type=f32).astype(bf16)
        out_up[:, cols] = jnp.dot(left, grads[1, :, cols], preferred_element_type=f32).astype(bf16)


def local(n_inp, n_outp, tokens, gate_pre, up_pre, grad_hidden, gate_weight, up_weight):
    rows, feats = tokens.shape
    trows, hid = gate_pre.shape
    half = hid // 2
    per = trows // rows
    every = n_outp * 2 * rows
    dma = pltpu.SemaphoreType.DMA
    anywhere = pl.BlockSpec(memory_space=pl.ANY)
    grad_tokens, grads, turned = pl.pallas_call(
        functools.partial(exchange, n_inp, n_outp),
        out_shape=(
            jax.ShapeDtypeStruct((rows, feats), bf16),
            jax.ShapeDtypeStruct((2, n_outp, 2, rows, half), bf16),
            jax.ShapeDtypeStruct((feats, every), bf16),
        ),
        in_specs=[anywhere] * 6,
        out_specs=(anywhere,) * 3,
        scratch_shapes=[
            pltpu.VMEM((trows, hid), bf16),
            pltpu.VMEM((trows, hid), bf16),
            pltpu.VMEM((trows, hid), bf16),
            pltpu.VMEM(gate_weight.shape, bf16),
            pltpu.VMEM(up_weight.shape, bf16),
            pltpu.VMEM((n_outp, 2, rows, feats), bf16),
            pltpu.VMEM((feats, every), bf16),
            pltpu.VMEM((2, n_outp, 2, rows, half), bf16),
            pltpu.VMEM((2, per, rows, half), bf16),
            pltpu.VMEM((n_outp, 2, rows, feats), f32),
            pltpu.VMEM((n_outp, 2, rows, feats), bf16),
            pltpu.VMEM((n_outp, rows, feats), bf16),
            pltpu.VMEM((n_outp, rows, feats), bf16),
            pltpu.VMEM((n_outp, rows, feats), bf16),
            pltpu.VMEM((rows, feats), bf16),
            dma((per, 3)), dma, dma((2,)),
            dma((n_outp,)), dma((n_outp,)), dma, dma,
            dma((n_inp, 2, per)), dma((n_inp, 2, per)),
            dma((n_outp,)), dma((n_outp,)),
            dma((n_outp,)), dma((n_outp,)),
            dma((n_outp,)), dma((2,)),
        ],
        compiler_params=pltpu.CompilerParams(
            collective_id=0, has_side_effects=True, vmem_limit_bytes=VMEM_BYTES
        ),
    )(tokens, gate_pre, up_pre, grad_hidden, gate_weight, up_weight)
    grads = grads.reshape(2, every, half)
    fw = width(feats)
    out_gate, out_up = pl.pallas_call(
        weight_grads,
        grid=(feats // fw,),
        out_shape=(jax.ShapeDtypeStruct((feats, half), bf16),) * 2,
        in_specs=[
            pl.BlockSpec((fw, every), lambda t: (t, 0)),
            pl.BlockSpec((2, every, half), lambda t: (0, 0, 0)),
        ],
        out_specs=(pl.BlockSpec((fw, half), lambda t: (t, 0)),) * 2,
        compiler_params=pltpu.CompilerParams(vmem_limit_bytes=VMEM_BYTES),
    )(turned, grads)
    return grad_tokens, out_gate, out_up


def solution(mesh):
    placed = (
        P(("groups", "depth", "outp"), "inp"),
        P(("groups", "depth", "inp"), "outp"),
        P(("groups", "depth", "inp"), "outp"),
        P(("groups", "depth", "inp"), "outp"),
        P("inp", ("outp", "depth")),
        P("inp", ("outp", "depth")),
    )
    return jax.shard_map(
        functools.partial(local, mesh.shape["inp"], mesh.shape["outp"]),
        mesh=mesh,
        in_specs=placed,
        out_specs=(
            P(("groups", "depth", "outp"), "inp"),
            P(("groups", "inp"), ("outp", "depth")),
            P(("groups", "inp"), ("outp", "depth")),
        ),
        check_vma=False,
    )
```

```python
import functools

import jax
import jax.numpy as jnp
from jax import lax
from jax.experimental import pallas as pl
from jax.experimental.pallas import tpu as pltpu
from jax.sharding import PartitionSpec as P

MESH = pl.DeviceIdType.MESH
f32, bf16 = jnp.float32, jnp.bfloat16
VMEM_BYTES = 60 * 1024 * 1024


def width(extent):
    return 256 if extent % 256 == 0 else 128


def exchange(
    n_inp, n_outp,
    tokens, gate, up, hidden, w_gate, w_up,
    out, grads_out, turned_out, *rest,
):
    tails = rest[:n_outp]
    (
        gv, uv, hv, wg, wu, tk, turned, gr, sb, pf, pb, xr, zs, zr, ov,
        in_sem, own_sem, w_sem, t_send, t_recv, f_send, f_recv,
        g_send, g_recv, x_send, x_recv, z_send, z_recv, o_sem, out_sem, tail_sem,
    ) = rest[n_outp:]
    i, o, d = lax.axis_index("inp"), lax.axis_index("outp"), lax.axis_index("depth")
    e = 1 - d
    per, parts, rows = gate.shape[:3]
    half = gate.shape[3] // 2
    feats = tokens.shape[2]
    oi, op = o // per, lax.rem(o, per)
    inps = [lax.rem(i + s, n_inp) for s in range(n_inp)]
    outps = [lax.rem(o + s, n_outp) for s in range(n_outp)]
    last = parts - 1

    loads = [
        [
            pltpu.make_async_copy(src.at[:, q], dst.at[:, q], in_sem.at[q, k])
            for k, (src, dst) in enumerate(((gate, gv), (up, uv), (hidden, hv)))
        ]
        for q in range(parts)
    ]
    own = pltpu.make_async_copy(tokens, tk.at[oi, :, op, d], own_sem)
    weights = [
        pltpu.make_async_copy(w_gate, wg, w_sem.at[0]),
        pltpu.make_async_copy(w_up, wu, w_sem.at[1]),
    ]
    for copy in loads[0] + [own] + sum(loads[1:], []) + weights:
        copy.start()

    barrier = pltpu.get_barrier_semaphore()
    for s in range(n_inp):
        for side in ((e,) if s == 0 else (d, e)):
            pl.semaphore_signal(barrier, inc=1, device_id={"inp": inps[s], "depth": side}, device_id_type=MESH)
    for s in range(1, n_outp):
        pl.semaphore_signal(barrier, inc=1, device_id={"outp": outps[s]}, device_id_type=MESH)
    pl.semaphore_wait(barrier, 2 * n_inp - 1 + n_outp - 1)

    cw = width(half)

    def pointwise(q, side, store):
        def step(c, carry):
            from_cols = pl.ds(pl.multiple_of(side * half + c * cw, cw), cw)
            cols = pl.ds(pl.multiple_of(c * cw, cw), cw)
            for p in range(per):
                g = gv[p, q, :, from_cols].astype(f32)
                u = uv[p, q, :, from_cols].astype(f32)
                h = hv[p, q, :, from_cols].astype(f32)
                sig = 1.0 / (1.0 + jnp.exp(-g))
                hs = h * sig
                store(p, cols, (hs * u * (1.0 + g * (1.0 - sig))).astype(bf16), (hs * g).astype(bf16))
            return carry
        lax.fori_loop(0, half // cw, step, 0)

    def grad_copy(q, s, far, src):
        return pltpu.make_async_remote_copy(
            src_ref=src, dst_ref=gr.at[:, i, q, :, d],
            send_sem=g_send.at[s, far, q], recv_sem=g_recv.at[i, d, q],
            device_id={"inp": inps[s], "depth": e if far else d}, device_id_type=MESH,
        )

    sends = []
    for q in range(parts):
        for copy in loads[q]:
            copy.wait()

        def store_there(p, cols, a, b):
            sb[0, q, p, :, cols] = a
            sb[1, q, p, :, cols] = b

        def store_here(p, cols, a, b):
            gr[0, i, q, p, d, :, cols] = a
            gr[1, i, q, p, d, :, cols] = b

        pointwise(q, e, store_there)
        for s in list(range(1, n_inp)) + [0]:
            copy = grad_copy(q, s, 1, sb.at[:, q])
            copy.start()
            sends.append(copy)
        pointwise(q, d, store_here)
        for s in range(1, n_inp):
            copy = grad_copy(q, s, 0, gr.at[:, i, q, :, d])
            copy.start()
            sends.append(copy)
        if q == 0:
            own.wait()
            for s in range(1, n_outp):
                copy = pltpu.make_async_remote_copy(
                    src_ref=tk.at[oi, :, op, d], dst_ref=tk.at[oi, :, op, d],
                    send_sem=t_send.at[s], recv_sem=t_recv.at[o],
                    device_id={"outp": outps[s]}, device_id_type=MESH,
                )
                copy.start()
                sends.append(copy)

    def arrival(slot, send_sem, recv_sem):
        return pltpu.make_async_remote_copy(
            src_ref=slot, dst_ref=slot, send_sem=send_sem, recv_sem=recv_sem,
            device_id={"depth": e}, device_id_type=MESH,
        )

    def await_grads(j, side, q):
        arrival(gr.at[:, j, q, :, side], g_send.at[0, 0, 0], g_recv.at[j, side, q]).wait_recv()

    fw = width(feats)

    def product(j, first, count):
        chosen = pl.ds(first, count)
        left_gate = gr[0, j, chosen].reshape(count * per * 2 * rows, half)
        left_up = gr[1, j, chosen].reshape(count * per * 2 * rows, half)

        def step(t, carry):
            cols = pl.ds(pl.multiple_of(t * fw, fw), fw)
            contract = (((1,), (1,)), ((), ()))
            acc = lax.dot_general(left_gate, wg[cols, :], contract, preferred_element_type=f32)
            acc = acc + lax.dot_general(left_up, wu[cols, :], contract, preferred_element_type=f32)
            acc = acc.reshape(count, per, 2, rows, fw)
            pf[j, chosen, :, :, :, cols] = acc
            pb[j, chosen, :, :, :, cols] = acc.astype(bf16)
            return carry
        lax.fori_loop(0, feats // fw, step, 0)

    def pair_copy(j, q):
        return pltpu.make_async_remote_copy(
            src_ref=pb.at[j, q, :, e], dst_ref=xr.at[j, q], send_sem=x_send.at[j, q], recv_sem=x_recv.at[j, q],
            device_id={"depth": e}, device_id_type=MESH,
        )

    def store_grads(j, q):
        return pltpu.make_async_copy(gr.at[:, j, q], grads_out.at[:, j, q], o_sem.at[j, q])

    def spread_copy(j, q, p):
        c = j * per + p
        return pltpu.make_async_remote_copy(
            src_ref=zs.at[j, q, p], dst_ref=zr.at[q, o], send_sem=z_send.at[q, c], recv_sem=z_recv.at[q, o],
            device_id={"outp": c}, device_id_type=MESH,
        )

    def tail_copy(j, p, k):
        return pltpu.make_async_copy(zs.at[j, last, p], tails[k], tail_sem.at[k])

    def begin(j, first, count):
        product(j, first, count)
        for q in range(first, first + count):
            pair_copy(j, q).start()
        for q in range(first, first + count):
            store_grads(j, q).start()

    def spread(j, q):
        pair_copy(j, q).wait_recv()
        for p in range(per):
            c = j * per + p
            zs[j, q, p] = (pf[j, q, p, d] + xr[j, q, p].astype(f32)).astype(bf16)
            if q == last:
                for k in range(n_outp):
                    @pl.when(lax.rem(c - o + n_outp, n_outp) == k)
                    def _():
                        tail_copy(j, p, k).start()
            else:
                @pl.when(c != o)
                def _():
                    spread_copy(j, q, p).start()

                @pl.when(c == o)
                def _():
                    zr[q, o] = zs[j, q, p]

    for q in range(parts):
        await_grads(i, e, q)
    for copy in weights:
        copy.wait()
    begin(i, 0, parts)
    for q in range(parts):
        spread(i, q)

    def take_tokens():
        for s in range(1, n_outp):
            c = outps[s]
            arrival(tk.at[c // per, :, lax.rem(c, per), d], t_send.at[0], t_recv.at[c]).wait_recv()
        onward = pltpu.make_async_remote_copy(
            src_ref=tk.at[:, :, :, d], dst_ref=tk.at[:, :, :, d], send_sem=f_send, recv_sem=f_recv,
            device_id={"depth": e}, device_id_type=MESH,
        )
        onward.start()
        arrival(tk.at[:, :, :, e], f_send, f_recv).wait_recv()

        def step(t, carry):
            cols = pl.ds(pl.multiple_of(t * fw, fw), fw)
            turned[cols, :] = tk[:, :, :, :, :, cols].reshape(turned.shape[1], fw).T
            return carry
        lax.fori_loop(0, feats // fw, step, 0)
        result = pltpu.make_async_copy(turned, turned_out, out_sem.at[0])
        result.start()
        return onward, result

    later = [(s, q) for q in range(parts) for s in range(1, n_inp)]
    onward = turned_copy = None
    for at, (s, q) in enumerate(later):
        if at == len(later) - 1:
            onward, turned_copy = take_tokens()
        for side in (d, e):
            await_grads(inps[s], side, q)
        begin(inps[s], q, 1)
        spread(inps[s], q)

    for q in range(last):
        for s in range(1, n_outp):
            arrival(zr.at[q, outps[s]], z_send.at[0, 0], z_recv.at[q, outps[s]]).wait_recv()

        def total(t, carry):
            cols = pl.ds(pl.multiple_of(t * fw, fw), fw)
            acc = zr[q, 0, :, cols].astype(f32)
            for c in range(1, n_outp):
                acc = acc + zr[q, c, :, cols].astype(f32)
            ov[q, :, cols] = acc.astype(bf16)
            return carry
        lax.fori_loop(0, feats // fw, total, 0)
    results = [turned_copy]
    if last:
        results.append(pltpu.make_async_copy(ov, out, out_sem.at[1]))
        results[-1].start()

    for copy in sends:
        copy.wait_send()
    onward.wait_send()
    for j in range(n_inp):
        for q in range(parts):
            pair_copy(j, q).wait_send()
            store_grads(j, q).wait()
            for p in range(per if q != last else 0):
                @pl.when(j * per + p != o)
                def _():
                    spread_copy(j, q, p).wait_send()
    for k in range(n_outp):
        tail_copy(0, 0, k).wait()
    for copy in results:
        copy.wait()


def weight_grads(turned, grads, out_gate, out_up):
    left = turned[...]
    cw = width(out_gate.shape[1])
    for c in range(out_gate.shape[1] // cw):
        cols = slice(c * cw, (c + 1) * cw)
        out_gate[:, cols] = jnp.dot(left, grads[0, :, cols], preferred_element_type=f32).astype(bf16)
        out_up[:, cols] = jnp.dot(left, grads[1, :, cols], preferred_element_type=f32).astype(bf16)


def local(n_inp, n_outp, tokens, gate_pre, up_pre, grad_hidden, gate_weight, up_weight):
    block, feats = tokens.shape
    trows, hid = gate_pre.shape
    half = hid // 2
    per = trows // block
    parts = 2 if block % 32 == 0 else 1
    rows = block // parts
    spread_parts = max(parts - 1, 1)
    every = n_outp * 2 * block
    dma = pltpu.SemaphoreType.DMA
    anywhere = pl.BlockSpec(memory_space=pl.ANY)
    cut = (per, parts, rows, hid)
    done, grads, turned, *tails = pl.pallas_call(
        functools.partial(exchange, n_inp, n_outp),
        out_shape=(
            jax.ShapeDtypeStruct((spread_parts, rows, feats), bf16),
            jax.ShapeDtypeStruct((2, n_inp, parts, per, 2, rows, half), bf16),
            jax.ShapeDtypeStruct((feats, every), bf16),
        ) + (jax.ShapeDtypeStruct((rows, feats), bf16),) * n_outp,
        in_specs=[anywhere] * 6,
        out_specs=(anywhere,) * (3 + n_outp),
        scratch_shapes=[
            pltpu.VMEM(cut, bf16),
            pltpu.VMEM(cut, bf16),
            pltpu.VMEM(cut, bf16),
            pltpu.VMEM(gate_weight.shape, bf16),
            pltpu.VMEM(up_weight.shape, bf16),
            pltpu.VMEM((n_inp, parts, per, 2, rows, feats), bf16),
            pltpu.VMEM((feats, every), bf16),
            pltpu.VMEM((2, n_inp, parts, per, 2, rows, half), bf16),
            pltpu.VMEM((2, parts, per, rows, half), bf16),
            pltpu.VMEM((n_inp, parts, per, 2, rows, feats), f32),
            pltpu.VMEM((n_inp, parts, per, 2, rows, feats), bf16),
            pltpu.VMEM((n_inp, parts, per, rows, feats), bf16),
            pltpu.VMEM((n_inp, parts, per, rows, feats), bf16),
            pltpu.VMEM((spread_parts, n_outp, rows, feats), bf16),
            pltpu.VMEM((spread_parts, rows, feats), bf16),
            dma((parts, 3)), dma, dma((2,)),
            dma((n_outp,)), dma((n_outp,)), dma, dma,
            dma((n_inp, 2, parts)), dma((n_inp, 2, parts)),
            dma((n_inp, parts)), dma((n_inp, parts)),
            dma((spread_parts, n_outp)), dma((spread_parts, n_outp)),
            dma((n_inp, parts)), dma((2,)), dma((n_outp,)),
        ],
        compiler_params=pltpu.CompilerParams(
            collective_id=0, has_side_effects=True, vmem_limit_bytes=VMEM_BYTES
        ),
    )(
        tokens.reshape(parts, rows, feats),
        gate_pre.reshape(cut), up_pre.reshape(cut), grad_hidden.reshape(cut),
        gate_weight, up_weight,
    )

    total = tails[0].astype(f32)
    for k in range(1, n_outp):
        shift = [(c, (c + k) % n_outp) for c in range(n_outp)]
        total = total + lax.ppermute(tails[k], "outp", shift).astype(f32)
    total = total.astype(bf16)
    grad_tokens = jnp.concatenate([done.reshape(-1, feats), total]) if parts > 1 else total

    grads = grads.reshape(2, every, half)
    fw = 640 if feats % 640 == 0 else width(feats)
    out_gate, out_up = pl.pallas_call(
        weight_grads,
        grid=(feats // fw,),
        out_shape=(jax.ShapeDtypeStruct((feats, half), bf16),) * 2,
        in_specs=[
            pl.BlockSpec((fw, every), lambda t: (t, 0)),
            pl.BlockSpec((2, every, half), lambda t: (0, 0, 0)),
        ],
        out_specs=(pl.BlockSpec((fw, half), lambda t: (t, 0)),) * 2,
        compiler_params=pltpu.CompilerParams(vmem_limit_bytes=VMEM_BYTES),
        cost_estimate=pl.CostEstimate(
            flops=4 * every * feats * half, bytes_accessed=6 * feats * half, transcendentals=0
        ),
    )(turned, grads)
    return grad_tokens, out_gate, out_up


def solution(mesh):
    placed = (
        P(("groups", "depth", "outp"), "inp"),
        P(("groups", "depth", "inp"), "outp"),
        P(("groups", "depth", "inp"), "outp"),
        P(("groups", "depth", "inp"), "outp"),
        P("inp", ("outp", "depth")),
        P("inp", ("outp", "depth")),
    )
    return jax.shard_map(
        functools.partial(local, mesh.shape["inp"], mesh.shape["outp"]),
        mesh=mesh,
        in_specs=placed,
        out_specs=(
            P(("groups", "depth", "outp"), "inp"),
            P(("groups", "inp"), ("outp", "depth")),
            P(("groups", "inp"), ("outp", "depth")),
        ),
        check_vma=False,
    )
```

```python
import functools

import jax
import jax.numpy as jnp
from jax import lax
from jax.experimental import pallas as pl
from jax.experimental.pallas import tpu as pltpu
from jax.sharding import PartitionSpec as P

MESH = pl.DeviceIdType.MESH
f32, bf16 = jnp.float32, jnp.bfloat16
VMEM_BYTES = 60 * 1024 * 1024
PIECES = 2


def width(extent):
    return 256 if extent % 256 == 0 else 128


def exchange(
    n_inp, n_outp,
    tokens, gate, up, hidden, w_gate, w_up,
    out, grads_out, turned_out, *rest,
):
    tails = rest[:n_outp]
    (
        gv, uv, hv, wg, wu, tk, turned, gr, sb, pf, pb, xr, zs, zr, ov,
        in_sem, own_sem, w_sem, t_send, t_recv, f_send, f_recv,
        g_send, g_recv, x_send, x_recv, z_send, z_recv, o_sem, out_sem, tail_sem,
    ) = rest[n_outp:]
    i, o, d = lax.axis_index("inp"), lax.axis_index("outp"), lax.axis_index("depth")
    e = 1 - d
    per, parts, rows = gate.shape[:3]
    half = gate.shape[3] // 2
    feats = tokens.shape[2]
    oi, op = o // per, lax.rem(o, per)
    inps = [lax.rem(i + s, n_inp) for s in range(n_inp)]
    outps = [lax.rem(o + s, n_outp) for s in range(n_outp)]
    last = parts - 1
    piece = half // PIECES

    loads = [
        [
            pltpu.make_async_copy(src.at[:, q], dst.at[:, q], in_sem.at[q, k])
            for k, (src, dst) in enumerate(((gate, gv), (up, uv), (hidden, hv)))
        ]
        for q in range(parts)
    ]
    own = pltpu.make_async_copy(tokens, tk.at[oi, :, op, d], own_sem)
    weights = [
        pltpu.make_async_copy(w_gate, wg, w_sem.at[0]),
        pltpu.make_async_copy(w_up, wu, w_sem.at[1]),
    ]
    for copy in loads[0] + [own] + sum(loads[1:], []) + weights:
        copy.start()

    barrier = pltpu.get_barrier_semaphore()
    for s in range(n_inp):
        for side in ((e,) if s == 0 else (d, e)):
            pl.semaphore_signal(barrier, inc=1, device_id={"inp": inps[s], "depth": side}, device_id_type=MESH)
    for s in range(1, n_outp):
        pl.semaphore_signal(barrier, inc=1, device_id={"outp": outps[s]}, device_id_type=MESH)

    cw = width(piece)

    def pointwise(q, side, store, begin, end):
        def step(c, carry):
            from_cols = pl.ds(pl.multiple_of(side * half + c * cw, cw), cw)
            cols = pl.ds(pl.multiple_of(c * cw, cw), cw)
            for p in range(per):
                g = gv[p, q, :, from_cols].astype(f32)
                u = uv[p, q, :, from_cols].astype(f32)
                h = hv[p, q, :, from_cols].astype(f32)
                sig = 1.0 / (1.0 + jnp.exp(-g))
                hs = h * sig
                store(p, cols, (hs * u * (1.0 + g * (1.0 - sig))).astype(bf16), (hs * g).astype(bf16))
            return carry
        lax.fori_loop(begin // cw, end // cw, step, 0)

    def spans(q):
        if q == last:
            return [(k * piece, (k + 1) * piece, last + k) for k in range(PIECES)]
        return [(0, half, q)]

    def grad_copy(q, s, far, span):
        begin, end, sem = span
        cols = pl.ds(begin, end - begin)
        slot = gr.at[:, i, q, :, d, :, cols]
        return pltpu.make_async_remote_copy(
            src_ref=sb.at[:, q, :, :, cols] if far else slot, dst_ref=slot,
            send_sem=g_send.at[s, far, sem], recv_sem=g_recv.at[i, d, sem],
            device_id={"inp": inps[s], "depth": e if far else d}, device_id_type=MESH,
        )

    sends = []
    for q in range(parts):
        for copy in loads[q]:
            copy.wait()

        def store_there(p, cols, a, b):
            sb[0, q, p, :, cols] = a
            sb[1, q, p, :, cols] = b

        def store_here(p, cols, a, b):
            gr[0, i, q, p, d, :, cols] = a
            gr[1, i, q, p, d, :, cols] = b

        for span in spans(q):
            pointwise(q, e, store_there, *span[:2])
            if not sends:
                pl.semaphore_wait(barrier, 2 * n_inp - 1 + n_outp - 1)
            for s in list(range(1, n_inp)) + [0]:
                copy = grad_copy(q, s, 1, span)
                copy.start()
                sends.append(copy)
            pointwise(q, d, store_here, *span[:2])
            for s in range(1, n_inp):
                copy = grad_copy(q, s, 0, span)
                copy.start()
                sends.append(copy)
        if q == 0:
            own.wait()
            for s in range(1, n_outp):
                copy = pltpu.make_async_remote_copy(
                    src_ref=tk.at[oi, :, op, d], dst_ref=tk.at[oi, :, op, d],
                    send_sem=t_send.at[s], recv_sem=t_recv.at[o],
                    device_id={"outp": outps[s]}, device_id_type=MESH,
                )
                copy.start()
                sends.append(copy)

    def arrival(slot, send_sem, recv_sem):
        return pltpu.make_async_remote_copy(
            src_ref=slot, dst_ref=slot, send_sem=send_sem, recv_sem=recv_sem,
            device_id={"depth": e}, device_id_type=MESH,
        )

    def await_grads(j, side, q, span):
        begin, end, sem = span
        slot = gr.at[:, j, q, :, side, :, pl.ds(begin, end - begin)]
        arrival(slot, g_send.at[0, 0, 0], g_recv.at[j, side, sem]).wait_recv()

    fw = width(feats)

    def product(j, first, count, begin, end):
        chosen, depth = pl.ds(first, count), pl.ds(begin, end - begin)
        left_gate = gr[0, j, chosen, :, :, :, depth].reshape(count * per * 2 * rows, end - begin)
        left_up = gr[1, j, chosen, :, :, :, depth].reshape(count * per * 2 * rows, end - begin)

        def step(t, carry):
            cols = pl.ds(pl.multiple_of(t * fw, fw), fw)
            contract = (((1,), (1,)), ((), ()))
            acc = lax.dot_general(left_gate, wg[cols, depth], contract, preferred_element_type=f32)
            acc = acc + lax.dot_general(left_up, wu[cols, depth], contract, preferred_element_type=f32)
            acc = acc.reshape(count, per, 2, rows, fw)
            if begin > 0:
                acc = acc + pf[j, chosen, :, :, :, cols]
            pf[j, chosen, :, :, :, cols] = acc
            if end == half:
                pb[j, chosen, :, :, :, cols] = acc.astype(bf16)
            return carry
        lax.fori_loop(0, feats // fw, step, 0)

    def pair_copy(j, q):
        return pltpu.make_async_remote_copy(
            src_ref=pb.at[j, q, :, e], dst_ref=xr.at[j, q], send_sem=x_send.at[j, q], recv_sem=x_recv.at[j, q],
            device_id={"depth": e}, device_id_type=MESH,
        )

    def store_grads(j, q):
        return pltpu.make_async_copy(gr.at[:, j, q], grads_out.at[:, j, q], o_sem.at[j, q])

    def spread_copy(j, q, p):
        c = j * per + p
        return pltpu.make_async_remote_copy(
            src_ref=zs.at[j, q, p], dst_ref=zr.at[q, o], send_sem=z_send.at[q, c], recv_sem=z_recv.at[q, o],
            device_id={"outp": c}, device_id_type=MESH,
        )

    def tail_copy(j, p, k):
        return pltpu.make_async_copy(zs.at[j, last, p], tails[k], tail_sem.at[k])

    def begin(j, first, count):
        for q in range(first, first + count):
            pair_copy(j, q).start()
        for q in range(first, first + count):
            store_grads(j, q).start()

    def spread(j, q):
        pair_copy(j, q).wait_recv()
        for p in range(per):
            c = j * per + p
            zs[j, q, p] = (pf[j, q, p, d] + xr[j, q, p].astype(f32)).astype(bf16)
            if q == last:
                for k in range(n_outp):
                    @pl.when(lax.rem(c - o + n_outp, n_outp) == k)
                    def _():
                        tail_copy(j, p, k).start()
            else:
                @pl.when(c != o)
                def _():
                    spread_copy(j, q, p).start()

                @pl.when(c == o)
                def _():
                    zr[q, o] = zs[j, q, p]

    for q in range(parts):
        for span in spans(q):
            await_grads(i, e, q, span)
    for copy in weights:
        copy.wait()
    product(i, 0, parts, 0, half)
    begin(i, 0, parts)
    for q in range(parts):
        spread(i, q)

    def take_tokens():
        for s in range(1, n_outp):
            c = outps[s]
            arrival(tk.at[c // per, :, lax.rem(c, per), d], t_send.at[0], t_recv.at[c]).wait_recv()
        onward = pltpu.make_async_remote_copy(
            src_ref=tk.at[:, :, :, d], dst_ref=tk.at[:, :, :, d], send_sem=f_send, recv_sem=f_recv,
            device_id={"depth": e}, device_id_type=MESH,
        )
        onward.start()
        return onward

    def turn_tokens():
        arrival(tk.at[:, :, :, e], f_send, f_recv).wait_recv()

        def step(t, carry):
            cols = pl.ds(pl.multiple_of(t * fw, fw), fw)
            turned[cols, :] = tk[:, :, :, :, :, cols].reshape(turned.shape[1], fw).T
            return carry
        lax.fori_loop(0, feats // fw, step, 0)
        result = pltpu.make_async_copy(turned, turned_out, out_sem.at[0])
        result.start()
        return result

    later = [(s, q) for q in range(parts) for s in range(1, n_inp)]
    onward = turned_copy = None
    for at, (s, q) in enumerate(later):
        if at == len(later) - 1:
            onward = take_tokens()
        for span in spans(q):
            for side in (d, e):
                await_grads(inps[s], side, q, span)
            product(inps[s], q, 1, span[0], span[1])
        begin(inps[s], q, 1)
        if at == len(later) - 1:
            turned_copy = turn_tokens()
        spread(inps[s], q)

    for q in range(last):
        for s in range(1, n_outp):
            arrival(zr.at[q, outps[s]], z_send.at[0, 0], z_recv.at[q, outps[s]]).wait_recv()

        def total(t, carry):
            cols = pl.ds(pl.multiple_of(t * fw, fw), fw)
            acc = zr[q, 0, :, cols].astype(f32)
            for c in range(1, n_outp):
                acc = acc + zr[q, c, :, cols].astype(f32)
            ov[q, :, cols] = acc.astype(bf16)
            return carry
        lax.fori_loop(0, feats // fw, total, 0)
    results = [turned_copy]
    if last:
        results.append(pltpu.make_async_copy(ov, out, out_sem.at[1]))
        results[-1].start()

    for copy in sends:
        copy.wait_send()
    onward.wait_send()
    for j in range(n_inp):
        for q in range(parts):
            pair_copy(j, q).wait_send()
            store_grads(j, q).wait()
            for p in range(per if q != last else 0):
                @pl.when(j * per + p != o)
                def _():
                    spread_copy(j, q, p).wait_send()
    for k in range(n_outp):
        tail_copy(0, 0, k).wait()
    for copy in results:
        copy.wait()


def weight_grads(turned, grads, out_gate, out_up):
    feats = turned.shape[0]
    tall = 512 if feats % 512 == 0 else feats
    for r in range(feats // tall):
        at = slice(r * tall, (r + 1) * tall)
        out_gate[at, :] = jnp.dot(turned[at, :], grads[0], preferred_element_type=f32).astype(bf16)
        out_up[at, :] = jnp.dot(turned[at, :], grads[1], preferred_element_type=f32).astype(bf16)


def local(n_inp, n_outp, tokens, gate_pre, up_pre, grad_hidden, gate_weight, up_weight):
    block, feats = tokens.shape
    trows, hid = gate_pre.shape
    half = hid // 2
    per = trows // block
    parts = 2 if block % 32 == 0 else 1
    rows = block // parts
    spread_parts = max(parts - 1, 1)
    every = n_outp * 2 * block
    dma = pltpu.SemaphoreType.DMA
    anywhere = pl.BlockSpec(memory_space=pl.ANY)
    cut = (per, parts, rows, hid)
    done, grads, turned, *tails = pl.pallas_call(
        functools.partial(exchange, n_inp, n_outp),
        out_shape=(
            jax.ShapeDtypeStruct((spread_parts, rows, feats), bf16),
            jax.ShapeDtypeStruct((2, n_inp, parts, per, 2, rows, half), bf16),
            jax.ShapeDtypeStruct((feats, every), bf16),
        ) + (jax.ShapeDtypeStruct((rows, feats), bf16),) * n_outp,
        in_specs=[anywhere] * 6,
        out_specs=(anywhere,) * (3 + n_outp),
        scratch_shapes=[
            pltpu.VMEM(cut, bf16),
            pltpu.VMEM(cut, bf16),
            pltpu.VMEM(cut, bf16),
            pltpu.VMEM(gate_weight.shape, bf16),
            pltpu.VMEM(up_weight.shape, bf16),
            pltpu.VMEM((n_inp, parts, per, 2, rows, feats), bf16),
            pltpu.VMEM((feats, every), bf16),
            pltpu.VMEM((2, n_inp, parts, per, 2, rows, half), bf16),
            pltpu.VMEM((2, parts, per, rows, half), bf16),
            pltpu.VMEM((n_inp, parts, per, 2, rows, feats), f32),
            pltpu.VMEM((n_inp, parts, per, 2, rows, feats), bf16),
            pltpu.VMEM((n_inp, parts, per, rows, feats), bf16),
            pltpu.VMEM((n_inp, parts, per, rows, feats), bf16),
            pltpu.VMEM((spread_parts, n_outp, rows, feats), bf16),
            pltpu.VMEM((spread_parts, rows, feats), bf16),
            dma((parts, 3)), dma, dma((2,)),
            dma((n_outp,)), dma((n_outp,)), dma, dma,
            dma((n_inp, 2, parts - 1 + PIECES)), dma((n_inp, 2, parts - 1 + PIECES)),
            dma((n_inp, parts)), dma((n_inp, parts)),
            dma((spread_parts, n_outp)), dma((spread_parts, n_outp)),
            dma((n_inp, parts)), dma((2,)), dma((n_outp,)),
        ],
        compiler_params=pltpu.CompilerParams(
            collective_id=0, has_side_effects=True, vmem_limit_bytes=VMEM_BYTES
        ),
    )(
        tokens.reshape(parts, rows, feats),
        gate_pre.reshape(cut), up_pre.reshape(cut), grad_hidden.reshape(cut),
        gate_weight, up_weight,
    )

    total = tails[0].astype(f32)
    for k in range(1, n_outp):
        shift = [(c, (c + k) % n_outp) for c in range(n_outp)]
        total = total + lax.ppermute(tails[k], "outp", shift).astype(f32)
    total = total.astype(bf16)
    grad_tokens = jnp.concatenate([done.reshape(-1, feats), total]) if parts > 1 else total

    grads = grads.reshape(2, every, half)
    cw = 512 if half % 512 == 0 else width(half)
    out_gate, out_up = pl.pallas_call(
        weight_grads,
        grid=(half // cw,),
        out_shape=(jax.ShapeDtypeStruct((feats, half), bf16),) * 2,
        in_specs=[
            pl.BlockSpec((feats, every), lambda t: (0, 0)),
            pl.BlockSpec((2, every, cw), lambda t: (0, 0, t)),
        ],
        out_specs=(pl.BlockSpec((feats, cw), lambda t: (0, t)),) * 2,
        compiler_params=pltpu.CompilerParams(vmem_limit_bytes=VMEM_BYTES),
        cost_estimate=pl.CostEstimate(
            flops=4 * every * feats * half, bytes_accessed=6 * feats * half, transcendentals=0
        ),
    )(turned, grads)
    return grad_tokens, out_gate, out_up


def solution(mesh):
    placed = (
        P(("groups", "depth", "outp"), "inp"),
        P(("groups", "depth", "inp"), "outp"),
        P(("groups", "depth", "inp"), "outp"),
        P(("groups", "depth", "inp"), "outp"),
        P("inp", ("outp", "depth")),
        P("inp", ("outp", "depth")),
    )
    return jax.shard_map(
        functools.partial(local, mesh.shape["inp"], mesh.shape["outp"]),
        mesh=mesh,
        in_specs=placed,
        out_specs=(
            P(("groups", "depth", "outp"), "inp"),
            P(("groups", "inp"), ("outp", "depth")),
            P(("groups", "inp"), ("outp", "depth")),
        ),
        check_vma=False,
    )
```
